256 devices in a mesh: dp: 16 (over x, y), context: 16 (over z, core).
Axes of the slice: x: 4, y: 4, z: 8, core: 2. Of those that a mesh axis runs over, the one named last changes fastest.
Arguments:
- queries: bfloat16 [65536, 512], P(('dp', 'context')), may hold values from -6 to 6
- keys: bfloat16 [65536, 128], P(('dp', 'context')), may hold values from -6 to 6
- values: bfloat16 [65536, 128], P(('dp', 'context')), may hold values from -6 to 6
- doc_ids: int32 [65536], P(('dp', 'context')), may hold values from 0 to 63, never falling along the last dimension, each value on 1 to 2048 neighbouring positions
Outputs:
- attended: bfloat16 [65536, 512], P(('dp', 'context'))
The draws below stay inside these ranges and needn't reach their ends.
Inputs may be any that keep to these rules, and one draw needn't show every extreme that they name: `doc_ids`: Non-decreasing along the tokens; no document has more than 2048 tokens, and one has exactly 2048.
All inputs are finite; a program needn't handle non-finite values.
Results may differ from the reference program's by a relative error of at most 0.0037.
Values may be sent and summed in bfloat16 or wider, within the bound.
No kernel may reach another device: no remote copies, remote signals or barrier semaphores. Data moves between devices by JAX's collectives and lax.ppermute only.
A program may use at most 128 MiB of HBM per device.

```python
import math
import jax
import jax.numpy as jnp
import numpy as np
from jax import lax

HEAD = 128
HEADS = 4
MAXDOC = 2048
TOKENS = 65536
DOCS = 64


def draw_keys(key, part):
    key = jax.random.fold_in(key, 11)
    rows = jnp.clip(jax.random.normal(key, (TOKENS, HEAD), jnp.float32), -6.0, 6.0)
    return rows.astype(jnp.bfloat16)


def draw_queries(key, part):
    key = jax.random.fold_in(key, 23)
    rows = jnp.clip(jax.random.normal(key, (TOKENS, HEADS * HEAD), jnp.float32), -6.0, 6.0)
    return rows.astype(jnp.bfloat16)


def block_scale(rng, dims, shards, smallest, high):
    def one(axis_at, parts):
        heights = jax.random.uniform(jax.random.fold_in(jax.random.fold_in(rng, 6), axis_at), (parts,), jnp.float32, smallest / len(shards), high / len(shards))
        return jnp.repeat(jnp.exp(heights), dims[axis_at] // parts).reshape((-1,) + (1,) * (len(dims) - axis_at - 1))

    level = one(*shards[0])
    for cut in shards[1:]:
        level = level * one(*cut)
    return level


def profile(amount, total, limit, slope):
    portions = [(1 << 20) // math.isqrt(standing ** slope) + 1 for standing in range(2, amount + 1)]
    surplus, holding = total - limit - (amount - 1), [1] * (amount - 1)
    while surplus > 0:
        free = [i for i in range(amount - 1) if holding[i] < limit]
        whole, left = sum([portions[i] for i in free]), surplus
        for i in free:
            addition = min(limit - holding[i], max(1, left * portions[i] // whole), surplus)
            holding[i] = holding[i] + addition
            surplus = surplus - addition
    return np.array([limit] + holding)


def ragged(own_key, count, total, most, slope):
    if count == 2:
        one = jax.random.randint(own_key, (), max(1, total - most), min(most, total - 1) + 1)
        return jnp.stack([one, total - one])
    tallies = jnp.asarray(profile(count, total, most, slope), jnp.int32)
    pairs = (count - 1) // 2
    source_of, receiver = tallies[1:1 + 2 * pairs:2], tallies[2:2 + 2 * pairs:2]
    slack = jnp.minimum(source_of - 1, most - receiver)
    shifted = jax.random.randint(jax.random.fold_in(own_key, 1), (pairs,), 0, 1 << 20) % (slack + 1)
    tallies = tallies.at[1:1 + 2 * pairs:2].set(source_of - shifted).at[2:2 + 2 * pairs:2].set(receiver + shifted)
    return tallies[jax.random.permutation(jax.random.fold_in(own_key, 2), count)]


def noise(stream_key, shape, deviation, reach, shards=(), kind=jnp.bfloat16):
    loudness = block_scale(stream_key, shape, shards, -0.22, 0.18) if shards else 1.0
    values = jax.random.normal(stream_key, shape, jnp.float32) * deviation * loudness
    return jnp.minimum(jnp.maximum(values, -reach), reach).astype(kind)


def setup_inputs(seed: int = 0) -> dict:
    splits = jax.random.split(jax.random.key(seed), 5)
    queries = draw_queries(jax.random.fold_in(splits[4], 71), 0)
    keys = draw_keys(jax.random.fold_in(splits[4], 71), 0)
    values = noise(splits[2], (TOKENS, HEAD), 1.0, 6.0, ((0, 256),))
    doc_ids = jnp.searchsorted(jnp.cumsum(ragged(splits[3], DOCS, TOKENS, MAXDOC, 0)), jnp.arange(TOKENS), side="right").astype(jnp.int32)
    return {"queries": queries, "keys": keys, "values": values, "doc_ids": doc_ids}


def reference(queries, keys, values, doc_ids):
    tokens = queries.shape[0]
    qblock = math.gcd(512, tokens)
    window = min(MAXDOC + qblock, tokens)
    scale = 1.0 / math.sqrt(HEAD)
    query_all = queries.reshape(tokens, HEADS, HEAD)

    def one_block(index):
        first = index * qblock
        key_first = jnp.clip(first - MAXDOC, 0, tokens - window).astype(jnp.int32)
        query_rows = lax.dynamic_slice_in_dim(query_all, first, qblock, 0)
        key_rows = lax.dynamic_slice_in_dim(keys, key_first, window, 0)
        value_rows = lax.dynamic_slice_in_dim(values, key_first, window, 0)
        query_ids = lax.dynamic_slice_in_dim(doc_ids, first, qblock, 0)
        key_ids = lax.dynamic_slice_in_dim(doc_ids, key_first, window, 0)
        query_pos = first + jnp.arange(qblock, dtype=jnp.int32)
        key_pos = key_first + jnp.arange(window, dtype=jnp.int32)
        allowed = (query_ids[:, None] == key_ids[None, :]) & (key_pos[None, :] <= query_pos[:, None])
        scores = jnp.einsum('qhd,kd->hqk', query_rows.astype(jnp.float32), key_rows.astype(jnp.float32)) * scale
        scores = jnp.where(allowed[None], scores, jnp.float32(-1e+30))
        top = lax.optimization_barrier(jnp.max(scores, axis=-1))
        raised = jnp.where(allowed[None], jnp.exp(scores - top[..., None]), jnp.float32(0.0))
        total = lax.optimization_barrier(jnp.sum(raised, axis=-1))
        weights = raised.astype(jnp.bfloat16)
        summed = jnp.einsum('hqk,kd->hqd', weights.astype(jnp.float32), value_rows.astype(jnp.float32))
        result = summed / total[..., None]
        return jnp.transpose(result, (1, 0, 2)).reshape(qblock, HEADS * HEAD).astype(jnp.bfloat16)
    blocks = lax.map(one_block, jnp.arange(tokens // qblock, dtype=jnp.int32))
    return blocks.reshape(tokens, HEADS * HEAD)
```

```python
import functools
import math

import jax
import jax.numpy as jnp
from jax import lax
from jax.experimental import pallas as pl
from jax.experimental.pallas import tpu as pltpu
from jax.sharding import PartitionSpec as P

outside = -2e30
lowest = -1e30
axes = ("dp", "context")
pad = 16


def chips_on(value, steps):
    count = lax.axis_size(axes[0]) * lax.axis_size(axes[1])
    shift = 2 * steps
    return lax.ppermute(value, axes, [(d, (d + shift) % count) for d in range(count)])


def both_cores(value):
    count = lax.axis_size("context")
    pairs = [[d, d + 1] for d in range(0, count, 2)]
    return lax.all_gather(value, "context", axis=0, tiled=True, axis_index_groups=pairs)


def core():
    return lax.rem(lax.axis_index("context"), 2)


def nt(a, b):
    return lax.dot_general(a, b, (((1,), (1,)), ((), ())), preferred_element_type=jnp.float32)


def nn(a, b):
    return lax.dot_general(a, b, (((1,), (0,)), ((), ())), preferred_element_type=jnp.float32)


def split(packed, rows, width):
    keys = packed[0:rows, 0:width]
    values = packed[0:rows, width : 2 * width].T
    ids = packed[rows : rows + 1, :].astype(jnp.float32)
    return keys, values, ids


def suffix_mask(ids, wanted, rows):
    matches = jnp.sum(jnp.where(ids == wanted, 1.0, 0.0), axis=1, keepdims=True)
    at = lax.broadcasted_iota(jnp.int32, (rows, rows), 0).astype(jnp.float32)
    return at >= rows - matches


def update(state, pieces, q, scale):
    top, total, acc = state
    scores = [jnp.where(mask, nt(keys, q) * scale, outside) for keys, _, mask in pieces]
    new_top = top
    for s in scores:
        new_top = jnp.maximum(new_top, jnp.max(s, axis=0, keepdims=True))
    fade = jnp.exp2(top - new_top)
    total = total * fade
    acc = acc * fade
    for s, (_, values, _) in zip(scores, pieces):
        raised = jnp.exp2(s - new_top)
        total = total + jnp.sum(raised, axis=0, keepdims=True)
        acc = acc + nn(values, raised.astype(jnp.bfloat16))
    return new_top, total, acc


def sides(q_ref, rows):
    mine = core()
    own = q_ref.at[pl.ds(pl.multiple_of(mine * rows, rows), rows), :]
    twin = q_ref.at[pl.ds(pl.multiple_of((1 - mine) * rows, rows), rows), :]
    return own, twin


def wanted_ids(own_ids, near_ids, rows):
    first = own_ids[:, 0:1]
    last = own_ids[:, rows - 1 : rows]
    near = near_ids[:, rows - 1 : rows]
    return first, jnp.where(core() == 0, last, near)


def early_kernel(scale, heads, q_ref, kv0_ref, kv1_ref, kv4_ref, stat_ref, acc_ref):
    rows, width = kv0_ref.shape[1], kv0_ref.shape[1] // 2
    own_q, twin_q = sides(q_ref, rows)
    keys0, values0, ids0 = split(kv0_ref, rows, width)
    keys1, values1, ids1 = split(kv1_ref, rows, width)
    keys4, values4, ids4 = split(kv4_ref, rows, width)
    first, other = wanted_ids(ids0, ids1, rows)
    at_key = lax.broadcasted_iota(jnp.int32, (rows, rows), 0)
    at_row = lax.broadcasted_iota(jnp.int32, (rows, rows), 1)
    ids_col = jnp.sum(jnp.where(at_key == at_row, ids0, 0.0), axis=1, keepdims=True)
    causal = (ids_col == ids0) & (at_key <= at_row)
    in_first = ids0 == first
    own = [
        (keys0, values0, causal),
        (keys1, values1, suffix_mask(ids1, first, rows) & in_first),
        (keys4, values4, suffix_mask(ids4, first, rows) & in_first),
    ]
    seen = jnp.where(core() == 0, ids0, -1.0)
    twin = [
        (keys0, values0, suffix_mask(seen, other, rows)),
        (keys1, values1, suffix_mask(ids1, other, rows)),
        (keys4, values4, suffix_mask(ids4, other, rows)),
    ]
    for side, (pieces, q) in enumerate(((own, own_q), (twin, twin_q))):
        for head in range(heads):
            state = (
                jnp.full((1, rows), lowest, jnp.float32),
                jnp.zeros((1, rows), jnp.float32),
                jnp.zeros((width, rows), jnp.float32),
            )
            q_head = q[:, head * width : (head + 1) * width]
            top, total, acc = update(state, pieces, q_head, scale)
            at = side * heads + head
            stat_ref[2 * at : 2 * at + 1, :] = top
            stat_ref[2 * at + 1 : 2 * at + 2, :] = total
            acc_ref[at * width : (at + 1) * width, :] = acc


def late_kernel(
    scale, heads, q_ref, kv0_ref, kv1_ref, kv2_ref, kv3_ref, stat_ref, acc_ref, lse_ref, mean_ref, send_ref
):
    rows, width = kv0_ref.shape[1], kv0_ref.shape[1] // 2
    own_q, twin_q = sides(q_ref, rows)
    ids0 = kv0_ref[rows : rows + 1, :].astype(jnp.float32)
    ids1 = kv1_ref[rows : rows + 1, :].astype(jnp.float32)
    keys2, values2, ids2 = split(kv2_ref, rows, width)
    keys3, values3, ids3 = split(kv3_ref, rows, width)
    first, other = wanted_ids(ids0, ids1, rows)
    in_first = ids0 == first
    own = [
        (keys2, values2, suffix_mask(ids2, first, rows) & in_first),
        (keys3, values3, suffix_mask(ids3, first, rows) & in_first),
    ]
    twin = [
        (keys2, values2, suffix_mask(ids2, other, rows)),
        (keys3, values3, suffix_mask(ids3, other, rows)),
    ]
    extra = []
    for side, (pieces, q) in enumerate(((twin, twin_q), (own, own_q))):
        for head in range(heads):
            at = (1 - side) * heads + head
            state = (
                stat_ref[2 * at : 2 * at + 1, :],
                stat_ref[2 * at + 1 : 2 * at + 2, :],
                acc_ref[at * width : (at + 1) * width, :],
            )
            q_head = q[:, head * width : (head + 1) * width]
            top, total, acc = update(state, pieces, q_head, scale)
            some = total > 0.0
            lse = jnp.where(some, top + jnp.log2(jnp.where(some, total, 1.0)), lowest)
            mean = acc * jnp.where(some, 1.0 / jnp.where(some, total, 1.0), 0.0)
            place = slice(head * width, (head + 1) * width)
            if side == 0:
                send_ref[place, :] = mean.astype(jnp.bfloat16)
                rest = lse
                for _ in range(3):
                    part = rest.astype(jnp.bfloat16)
                    extra.append(part.astype(jnp.float32))
                    rest = rest - part.astype(jnp.float32)
            else:
                lse_ref[head : head + 1, :] = lse
                mean_ref[place, :] = mean
    extra.append(jnp.broadcast_to(other, (1, rows)))
    extra.append(jnp.zeros((pad - len(extra), rows), jnp.float32))
    send_ref[heads * width :, :] = jnp.concatenate(extra, axis=0).astype(jnp.bfloat16)


def merge_kernel(heads, kv0_ref, lse_ref, mean_ref, sent_ref, out_ref):
    rows, width = kv0_ref.shape[1], kv0_ref.shape[1] // 2
    ids0 = kv0_ref[rows : rows + 1, :].astype(jnp.float32)
    first = ids0[:, 0:1]
    height = heads * width + pad
    start = pl.multiple_of((1 - core()) * height, pad)
    theirs = sent_ref.at[pl.ds(start, height), :]
    extra = theirs[heads * width :, :].astype(jnp.float32)
    usable = (ids0 == first) & (extra[3 * heads : 3 * heads + 1, :] == first)
    for head in range(heads):
        lse = lse_ref[head : head + 1, :]
        their = (
            extra[3 * head : 3 * head + 1, :]
            + extra[3 * head + 1 : 3 * head + 2, :]
            + extra[3 * head + 2 : 3 * head + 3, :]
        )
        their = jnp.where(usable, their, lowest)
        high = jnp.maximum(lse, their)
        a = jnp.exp2(lse - high)
        b = jnp.exp2(their - high)
        share = 1.0 / (a + b)
        place = slice(head * width, (head + 1) * width)
        merged = mean_ref[place, :] * (a * share) + theirs[place, :].astype(jnp.float32) * (b * share)
        out_ref[:, place] = merged.T.astype(jnp.bfloat16)


def call(kernel, outs, flops, *args):
    vmem = pl.BlockSpec(memory_space=pltpu.VMEM)
    moved = sum(math.prod(a.shape) * a.dtype.itemsize for a in (*args, *outs))
    return pl.pallas_call(
        kernel,
        out_shape=outs,
        in_specs=[vmem] * len(args),
        out_specs=[vmem] * len(outs),
        cost_estimate=pl.CostEstimate(flops=flops, bytes_accessed=moved, transcendentals=flops // 512),
        compiler_params=pltpu.CompilerParams(vmem_limit_bytes=40 * 2**20),
    )(*args)


def body(queries, keys, values, doc_ids):
    rows, width = keys.shape
    heads = queries.shape[1] // width
    scale = math.log2(math.e) / math.sqrt(width)
    ids = jnp.broadcast_to(doc_ids.astype(jnp.bfloat16)[None, :], (pad, rows))
    kv0 = jnp.concatenate([jnp.concatenate([keys, values], axis=1), ids], axis=0)
    kv4 = chips_on(kv0, 4)
    kv1 = chips_on(kv0, 1)
    kv2 = chips_on(kv0, 2)
    kv3 = chips_on(kv4, -1)
    q_chip = both_cores(queries)
    f32, bf16 = jnp.float32, jnp.bfloat16
    unit = 4 * heads * rows * rows * width
    stat, acc = call(
        functools.partial(early_kernel, scale, heads),
        [
            jax.ShapeDtypeStruct((4 * heads, rows), f32),
            jax.ShapeDtypeStruct((2 * heads * width, rows), f32),
        ],
        6 * unit,
        q_chip,
        kv0,
        kv1,
        kv4,
    )
    lse, mean, send = call(
        functools.partial(late_kernel, scale, heads),
        [
            jax.ShapeDtypeStruct((8, rows), f32),
            jax.ShapeDtypeStruct((heads * width, rows), f32),
            jax.ShapeDtypeStruct((heads * width + pad, rows), bf16),
        ],
        4 * unit,
        q_chip,
        kv0,
        kv1,
        kv2,
        kv3,
        stat,
        acc,
    )
    sent = both_cores(send)
    (out,) = call(
        functools.partial(merge_kernel, heads),
        [jax.ShapeDtypeStruct((rows, heads * width), bf16)],
        unit // 64,
        kv0,
        lse,
        mean,
        sent,
    )
    return out


def solution(mesh):
    split_spec = P(axes, None)
    return jax.shard_map(
        body,
        mesh=mesh,
        in_specs=(split_spec, split_spec, split_spec, P(axes)),
        out_specs=split_spec,
        check_vma=False,
    )
```

```python
import functools
import math

import jax
import jax.numpy as jnp
from jax import lax
from jax.experimental import pallas as pl
from jax.experimental.pallas import tpu as pltpu
from jax.sharding import PartitionSpec as P

outside = -1e30
axes = ("dp", "context")
pad = 8


def chips_on(value, steps, wrap):
    count = lax.axis_size(axes[0]) * lax.axis_size(axes[1])
    shift = 2 * steps
    pairs = [(d, (d + shift) % count) for d in range(count)]
    return lax.ppermute(value, axes, [(a, b) for a, b in pairs if wrap or b == a + shift])


def other_core(value):
    count = lax.axis_size(axes[0]) * lax.axis_size(axes[1])
    return lax.ppermute(value, axes, [(d, d ^ 1) for d in range(count)])


def pack(keys, values, doc_ids):
    rows = keys.shape[0]
    packed = jnp.pad(jnp.concatenate([keys, values], axis=1), ((0, pad), (0, 0)))
    packed, doc_ids = lax.optimization_barrier((packed, doc_ids))
    ids = jnp.broadcast_to((doc_ids + 1).astype(jnp.bfloat16)[None, :], (pad, rows))
    return lax.dynamic_update_slice(packed, ids, (rows, 0))


def nt(a, b):
    return lax.dot_general(a, b, (((1,), (1,)), ((), ())), preferred_element_type=jnp.float32)


def nn(a, b):
    return lax.dot_general(a, b, (((1,), (0,)), ((), ())), preferred_element_type=jnp.float32)


def iotas(rows, columns):
    down = lax.broadcasted_iota(jnp.int32, (rows, columns), 0)
    across = lax.broadcasted_iota(jnp.int32, (rows, columns), 1)
    return down, across


def ids_of(ref):
    rows = ref.shape[1]
    return ref[rows : rows + 1, :].astype(jnp.float32)


def count(ids, wanted):
    return jnp.sum(jnp.where(ids == wanted, 1.0, 0.0), axis=1, keepdims=True)


def on_core_one():
    return jnp.where(lax.rem(lax.axis_index("context"), 2) == 1, 1.0, 0.0)


def causal_mask(own_ref):
    rows = own_ref.shape[1]
    ids = ids_of(own_ref)
    at_row, at_key = iotas(rows, rows)
    ids_col = jnp.sum(jnp.where(at_key == at_row, ids, 0.0), axis=1, keepdims=True)
    return (ids_col == ids) & (at_key <= at_row)


def wide_keys(ref, first, keep):
    rows, width = ref.shape[1], ref.shape[1] // 2
    matches = count(ids_of(ref), first) * keep
    down, across = iotas(rows, width)
    masked = jnp.where(down.astype(jnp.float32) >= rows - matches, 0.0, outside)
    extra = jnp.where(across == 0, masked, jnp.where(across == 1, 1.0, 0.0))
    return jnp.concatenate([ref[0:rows, 0:width], extra.astype(jnp.bfloat16)], axis=1)


def wide_values(ref):
    rows, width = ref.shape[1], ref.shape[1] // 2
    return jnp.concatenate([ref[0:rows, width : 2 * width], jnp.ones((rows, width), jnp.bfloat16)], axis=1)


def query_extra(ids, first, rows, width):
    down, across = iotas(rows, width)
    in_first = jnp.where(down.astype(jnp.float32) < count(ids, first), 0.0, outside)
    return jnp.where(across == 0, 1.0, jnp.where(across == 1, in_first, 0.0)).astype(jnp.bfloat16)


def attend_kernel(scale, heads, begin, end, n_pieces, q_ref, own_ref, *refs):
    rows, width = own_ref.shape[1], own_ref.shape[1] // 2
    piece_refs, refs = refs[:n_pieces], refs[n_pieces:]
    if begin:
        q_out, top_out, acc_out, keys_ref, values_ref = refs
    elif end:
        top_in, acc_in, out_ref, keys_ref, values_ref, done_ref, sems = refs
    else:
        top_in, acc_in, top_out, acc_out, keys_ref, values_ref = refs
    ids = ids_of(own_ref)
    first = ids[:, 0:1]
    if begin:
        causal = causal_mask(own_ref)
        own_keys, own_values = own_ref[0:rows, 0:width], wide_values(own_ref)
        extra = query_extra(ids, first, rows, width)
    for at, ref in enumerate(piece_refs):
        here = slice(at * rows, (at + 1) * rows)
        keys_ref[here, :] = wide_keys(ref, first, on_core_one() if begin and at == 0 else 1.0)
        values_ref[here, :] = wide_values(ref)
    copies = []
    for head in range(heads):
        here = slice(head * rows, (head + 1) * rows)
        place = slice(head * width, (head + 1) * width)
        if begin:
            q = q_ref[:, place]
            wide = jnp.concatenate([q, extra], axis=1)
            q_out[here, :] = wide
            own_scores = jnp.where(causal, nt(q, own_keys), outside)
            before = jnp.max(own_scores, axis=1, keepdims=True)
        else:
            wide = q_ref[here, :]
            before = top_in[here, 0:1]
        scores = nt(wide, keys_ref[...])
        top = jnp.maximum(before, jnp.max(scores, axis=1, keepdims=True))
        acc = nn(jnp.exp2((scores - top) * scale).astype(jnp.bfloat16), values_ref[...])
        if begin:
            acc = acc + nn(jnp.exp2((own_scores - top) * scale).astype(jnp.bfloat16), own_values)
        else:
            acc = acc + acc_in[here, :] * jnp.exp2((before - top) * scale)
        if end:
            done_ref[:, place] = (acc[:, 0:width] / acc[:, width:]).astype(jnp.bfloat16)
            copy = pltpu.make_async_copy(done_ref.at[:, place], out_ref.at[:, place], sems.at[head])
            copy.start()
            copies.append(copy)
        else:
            top_out[here, :] = jnp.broadcast_to(top, (rows, width))
            acc_out[here, :] = acc
    for copy in copies:
        copy.wait()


def call(scale, heads, begin, end, q, own, pieces, state):
    vmem = pl.BlockSpec(memory_space=pltpu.VMEM)
    rows, width = own.shape[1], own.shape[1] // 2
    shape, f32, bf16 = jax.ShapeDtypeStruct, jnp.float32, jnp.bfloat16
    outs = [shape((heads * rows, width), f32), shape((heads * rows, 2 * width), f32)]
    if begin:
        outs.insert(0, shape((heads * rows, 2 * width), bf16))
    scratch = [pltpu.VMEM((len(pieces) * rows, 2 * width), bf16)] * 2
    out_specs = [vmem] * len(outs)
    if end:
        outs, out_specs = [shape((rows, heads * width), bf16)], [pl.BlockSpec(memory_space=pl.ANY)]
        scratch += [pltpu.VMEM((rows, heads * width), bf16), pltpu.SemaphoreType.DMA((heads,))]
    args = (q, own, *pieces, *state)
    moved = sum(math.prod(a.shape) * a.dtype.itemsize for a in (*args, *outs))
    flops = 8 * (len(pieces) + begin) * heads * rows * rows * width
    return pl.pallas_call(
        functools.partial(attend_kernel, scale, heads, begin, end, len(pieces)),
        out_shape=outs,
        in_specs=[vmem] * len(args),
        out_specs=out_specs,
        scratch_shapes=scratch,
        cost_estimate=pl.CostEstimate(flops=flops, bytes_accessed=moved, transcendentals=flops // 512),
        compiler_params=pltpu.CompilerParams(vmem_limit_bytes=40 * 2**20),
    )(*args)


def body(queries, keys, values, doc_ids):
    heads = queries.shape[1] // keys.shape[1]
    scale = math.log2(math.e) / math.sqrt(keys.shape[1])
    kv0 = pack(keys, values, doc_ids)
    kv4 = chips_on(kv0, 4, True)
    kv2 = chips_on(kv0, 2, False)
    kv1 = chips_on(kv0, 1, False)
    kv3 = chips_on(kv4, -1, True)
    attend = functools.partial(call, scale, heads)

    def both(piece):
        return [piece, other_core(piece)]

    kv4t = other_core(kv4)
    q, *state = attend(True, False, queries, kv0, [other_core(kv0), kv4], [])
    q, state, kv1 = lax.optimization_barrier((q, state, kv1))
    state = attend(False, False, q, kv0, [*both(kv1), kv4t], state)
    (out,) = attend(False, True, q, kv0, [*both(kv2), *both(kv3)], state)
    return out


def solution(mesh):
    split_spec = P(axes, None)
    return jax.shard_map(
        body,
        mesh=mesh,
        in_specs=(split_spec, split_spec, split_spec, P(axes)),
        out_specs=split_spec,
        check_vma=False,
    )
```

```python
import functools
import math

import jax
import jax.numpy as jnp
from jax import lax
from jax.experimental import pallas as pl
from jax.experimental.pallas import tpu as pltpu
from jax.sharding import PartitionSpec as P

outside = -1e30
axes = ("dp", "context")
pad = 8


def chips_on(value, steps, wrap):
    count = lax.axis_size(axes[0]) * lax.axis_size(axes[1])
    shift = 2 * steps
    pairs = [(d, (d + shift) % count) for d in range(count)]
    return lax.ppermute(value, axes, [(a, b) for a, b in pairs if wrap or b == a + shift])


def other_core(value):
    count = lax.axis_size(axes[0]) * lax.axis_size(axes[1])
    return lax.ppermute(value, axes, [(d, d ^ 1) for d in range(count)])


def pack(keys, values, doc_ids):
    rows = keys.shape[0]
    packed = jnp.pad(jnp.concatenate([keys, values], axis=1), ((0, pad), (0, 0)))
    packed, doc_ids = lax.optimization_barrier((packed, doc_ids))
    ids = jnp.broadcast_to((doc_ids + 1).astype(jnp.bfloat16)[None, :], (pad, rows))
    return lax.dynamic_update_slice(packed, ids, (rows, 0))


def nt(a, b):
    return lax.dot_general(a, b, (((1,), (1,)), ((), ())), preferred_element_type=jnp.float32)


def nn(a, b):
    return lax.dot_general(a, b, (((1,), (0,)), ((), ())), preferred_element_type=jnp.float32)


def iotas(rows, columns):
    down = lax.broadcasted_iota(jnp.int32, (rows, columns), 0)
    across = lax.broadcasted_iota(jnp.int32, (rows, columns), 1)
    return down, across


def ids_of(ref):
    rows = ref.shape[1]
    return ref[rows : rows + 1, :].astype(jnp.float32)


def count(ids, wanted):
    return jnp.sum(jnp.where(ids == wanted, 1.0, 0.0), axis=1, keepdims=True)


def on_core_one():
    return jnp.where(lax.rem(lax.axis_index("context"), 2) == 1, 1.0, 0.0)


def causal_mask(own_ref):
    rows = own_ref.shape[1]
    ids = ids_of(own_ref)
    at_row, at_key = iotas(rows, rows)
    ids_col = jnp.sum(jnp.where(at_key == at_row, ids, 0.0), axis=1, keepdims=True)
    return (ids_col == ids) & (at_key <= at_row)


def wide_keys(ref, first, keep):
    rows, width = ref.shape[1], ref.shape[1] // 2
    matches = count(ids_of(ref), first) * keep
    down, across = iotas(rows, width)
    masked = jnp.where(down.astype(jnp.float32) >= rows - matches, 0.0, outside)
    extra = jnp.where(across == 0, masked, jnp.where(across == 1, 1.0, 0.0))
    return jnp.concatenate([ref[0:rows, 0:width], extra.astype(jnp.bfloat16)], axis=1)


def wide_values(ref):
    rows, width = ref.shape[1], ref.shape[1] // 2
    return jnp.concatenate([ref[0:rows, width : 2 * width], jnp.ones((rows, width), jnp.bfloat16)], axis=1)


def query_extra(ids, first, rows, width):
    down, across = iotas(rows, width)
    in_first = jnp.where(down.astype(jnp.float32) < count(ids, first), 0.0, outside)
    return jnp.where(across == 0, 1.0, jnp.where(across == 1, in_first, 0.0)).astype(jnp.bfloat16)


def first_kernel(scale, heads, q_ref, own_ref, *refs):
    *piece_refs, q_out, top_out, acc_out, keys_ref, values_ref = refs
    rows, width = own_ref.shape[1], own_ref.shape[1] // 2
    ids = ids_of(own_ref)
    first = ids[:, 0:1]
    causal = causal_mask(own_ref)
    own_keys, own_values = own_ref[0:rows, 0:width], wide_values(own_ref)
    extra = query_extra(ids, first, rows, width)
    for at, ref in enumerate(piece_refs):
        here = slice(at * rows, (at + 1) * rows)
        keys_ref[here, :] = wide_keys(ref, first, on_core_one() if at == 0 else 1.0)
        values_ref[here, :] = wide_values(ref)
    for head in range(heads):
        here = slice(head * rows, (head + 1) * rows)
        q = q_ref[:, head * width : (head + 1) * width]
        wide = jnp.concatenate([q, extra], axis=1)
        q_out[here, :] = wide
        own_scores = jnp.where(causal, nt(q, own_keys), outside)
        scores = nt(wide, keys_ref[...])
        top = jnp.maximum(jnp.max(own_scores, axis=1, keepdims=True), jnp.max(scores, axis=1, keepdims=True))
        acc = nn(jnp.exp2((own_scores - top) * scale).astype(jnp.bfloat16), own_values)
        acc = acc + nn(jnp.exp2((scores - top) * scale).astype(jnp.bfloat16), values_ref[...])
        top_out[here, :] = jnp.broadcast_to(top, (rows, width))
        acc_out[here, :] = acc


def next_kernel(scale, heads, end, sizes, q_ref, own_ref, *refs):
    n_pieces = sum(sizes)
    piece_refs, refs = refs[:n_pieces], refs[n_pieces:]
    if end:
        top_in, acc_in, out_ref, keys_ref, values_ref, done_ref, sems = refs
    else:
        top_in, acc_in, top_out, acc_out, keys_ref, values_ref = refs
    rows, width = own_ref.shape[1], own_ref.shape[1] // 2
    first = ids_of(own_ref)[:, 0:1]
    level, at = jnp.zeros((1, 1), jnp.int32), 0
    for step, size in enumerate(sizes):
        matches = sum(count(ids_of(ref), first) for ref in piece_refs[at : at + size])
        level = jnp.where(matches > 0.0, step + 1, level)
        at += size
    level = level[0, 0]

    def go(n):
        for at, ref in enumerate(piece_refs[:n]):
            here = slice(at * rows, (at + 1) * rows)
            keys_ref[here, :] = wide_keys(ref, first, 1.0)
            values_ref[here, :] = wide_values(ref)
        copies = []
        for head in range(heads):
            here = slice(head * rows, (head + 1) * rows)
            place = slice(head * width, (head + 1) * width)
            acc = acc_in[here, :]
            if n:
                before = top_in[here, 0:1]
                scores = nt(q_ref[here, :], keys_ref[0 : n * rows, :])
                top = jnp.maximum(before, jnp.max(scores, axis=1, keepdims=True))
                acc = acc * jnp.exp2((before - top) * scale)
                acc = acc + nn(jnp.exp2((scores - top) * scale).astype(jnp.bfloat16), values_ref[0 : n * rows, :])
            if end:
                done_ref[:, place] = (acc[:, 0:width] / acc[:, width:]).astype(jnp.bfloat16)
                copy = pltpu.make_async_copy(done_ref.at[:, place], out_ref.at[:, place], sems.at[head])
                copy.start()
                copies.append(copy)
            else:
                top_out[here, :] = jnp.broadcast_to(top, (rows, width))
                acc_out[here, :] = acc
        for copy in copies:
            copy.wait()

    if not end:
        return go(n_pieces)
    for step in range(len(sizes) + 1):
        pl.when(level == step)(functools.partial(go, sum(sizes[:step])))


def call(scale, heads, begin, end, q, own, sizes, pieces, state):
    vmem = pl.BlockSpec(memory_space=pltpu.VMEM)
    rows, width = own.shape[1], own.shape[1] // 2
    shape, f32, bf16 = jax.ShapeDtypeStruct, jnp.float32, jnp.bfloat16
    outs = [shape((heads * rows, width), f32), shape((heads * rows, 2 * width), f32)]
    kernel = functools.partial(next_kernel, scale, heads, end, sizes)
    if begin:
        outs.insert(0, shape((heads * rows, 2 * width), bf16))
        kernel = functools.partial(first_kernel, scale, heads)
    scratch = [pltpu.VMEM((len(pieces) * rows, 2 * width), bf16)] * 2
    out_specs = [vmem] * len(outs)
    if end:
        outs, out_specs = [shape((rows, heads * width), bf16)], [pl.BlockSpec(memory_space=pl.ANY)]
        scratch += [pltpu.VMEM((rows, heads * width), bf16), pltpu.SemaphoreType.DMA((heads,))]
    args = (q, own, *pieces, *state)
    moved = sum(math.prod(a.shape) * a.dtype.itemsize for a in (*args, *outs))
    flops = 8 * (len(pieces) + begin) * heads * rows * rows * width
    return pl.pallas_call(
        kernel,
        out_shape=outs,
        in_specs=[vmem] * len(args),
        out_specs=out_specs,
        scratch_shapes=scratch,
        cost_estimate=pl.CostEstimate(flops=flops, bytes_accessed=moved, transcendentals=flops // 512),
        compiler_params=pltpu.CompilerParams(vmem_limit_bytes=40 * 2**20),
    )(*args)


def body(queries, keys, values, doc_ids):
    heads = queries.shape[1] // keys.shape[1]
    scale = math.log2(math.e) / math.sqrt(keys.shape[1])
    kv0 = pack(keys, values, doc_ids)
    kv4 = chips_on(kv0, 4, True)
    kv2 = chips_on(kv0, 2, False)
    kv1 = chips_on(kv0, 1, True)
    kv3 = chips_on(kv4, -1, True)
    attend = functools.partial(call, scale, heads)

    def both(piece):
        return [piece, other_core(piece)]

    kv4t = other_core(kv4)
    q, *state = attend(True, False, queries, kv0, (2,), [other_core(kv0), kv4], [])
    q, state, kv1 = lax.optimization_barrier((q, state, kv1))
    state = attend(False, False, q, kv0, (2, 1), [*both(kv1), kv4t], state)
    (out,) = attend(False, True, q, kv0, (2, 2), [*both(kv2), *both(kv3)], state)
    return out


def solution(mesh):
    split_spec = P(axes, None)
    return jax.shard_map(
        body,
        mesh=mesh,
        in_specs=(split_spec, split_spec, split_spec, P(axes)),
        out_specs=split_spec,
        check_vma=False,
    )
```

```python
import functools
import math

import jax
import jax.numpy as jnp
from jax import lax
from jax.experimental import pallas as pl
from jax.experimental.pallas import tpu as pltpu
from jax.sharding import PartitionSpec as P

outside = -1e30
axes = ("dp", "context")
pad = 8


def chips_on(value, steps, wrap):
    count = lax.axis_size(axes[0]) * lax.axis_size(axes[1])
    shift = 2 * steps
    pairs = [(d, (d + shift) % count) for d in range(count)]
    return lax.ppermute(value, axes, [(a, b) for a, b in pairs if wrap or b == a + shift])


def other_core(value):
    count = lax.axis_size(axes[0]) * lax.axis_size(axes[1])
    return lax.ppermute(value, axes, [(d, d ^ 1) for d in range(count)])


def pack(keys, values, doc_ids):
    rows = keys.shape[0]
    packed = jnp.pad(jnp.concatenate([keys, values], axis=1), ((0, pad), (0, 0)))
    packed, doc_ids = lax.optimization_barrier((packed, doc_ids))
    ids = jnp.broadcast_to((doc_ids + 1).astype(jnp.bfloat16)[None, :], (pad, rows))
    return lax.dynamic_update_slice(packed, ids, (rows, 0))


def nt(a, b):
    return lax.dot_general(a, b, (((1,), (1,)), ((), ())), preferred_element_type=jnp.float32)


def nn(a, b):
    return lax.dot_general(a, b, (((1,), (0,)), ((), ())), preferred_element_type=jnp.float32)


def iotas(rows, columns):
    down = lax.broadcasted_iota(jnp.int32, (rows, columns), 0)
    across = lax.broadcasted_iota(jnp.int32, (rows, columns), 1)
    return down, across


def ids_of(ref):
    rows = ref.shape[1]
    return ref[rows : rows + 1, :].astype(jnp.float32)


def count(ids, wanted):
    return jnp.sum(jnp.where(ids == wanted, 1.0, 0.0), axis=1, keepdims=True)


def on_core_one():
    return jnp.where(lax.rem(lax.axis_index("context"), 2) == 1, 1.0, 0.0)


def causal_mask(own_ref):
    rows = own_ref.shape[1]
    ids = ids_of(own_ref)
    at_row, at_key = iotas(rows, rows)
    ids_col = jnp.sum(jnp.where(at_key == at_row, ids, 0.0), axis=1, keepdims=True)
    return (ids_col == ids) & (at_key <= at_row)


def wide_keys(ref, first, keep):
    rows, width = ref.shape[1], ref.shape[1] // 2
    matches = count(ids_of(ref), first) * keep
    down, across = iotas(rows, width)
    masked = jnp.where(down.astype(jnp.float32) >= rows - matches, 0.0, outside)
    extra = jnp.where(across == 0, masked, jnp.where(across == 1, 1.0, 0.0))
    return jnp.concatenate([ref[0:rows, 0:width], extra.astype(jnp.bfloat16)], axis=1)


def wide_values(ref):
    rows, width = ref.shape[1], ref.shape[1] // 2
    return jnp.concatenate([ref[0:rows, width : 2 * width], jnp.ones((rows, width), jnp.bfloat16)], axis=1)


def query_extra(ids, first, rows, width):
    down, across = iotas(rows, width)
    in_first = jnp.where(down.astype(jnp.float32) < count(ids, first), 0.0, outside)
    return jnp.where(across == 0, 1.0, jnp.where(across == 1, in_first, 0.0)).astype(jnp.bfloat16)


def first_kernel(scale, heads, q_ref, own_ref, *refs):
    *piece_refs, q_out, top_out, acc_out, keys_ref, values_ref = refs
    rows, width = own_ref.shape[1], own_ref.shape[1] // 2
    ids = ids_of(own_ref)
    first = ids[:, 0:1]
    causal = causal_mask(own_ref)
    own_keys, own_values = own_ref[0:rows, 0:width], wide_values(own_ref)
    extra = query_extra(ids, first, rows, width)
    for at, ref in enumerate(piece_refs):
        here = slice(at * rows, (at + 1) * rows)
        keys_ref[here, :] = wide_keys(ref, first, on_core_one() if at == 0 else 1.0)
        values_ref[here, :] = wide_values(ref)
    for head in range(heads):
        here = slice(head * rows, (head + 1) * rows)
        q = q_ref[:, head * width : (head + 1) * width]
        wide = jnp.concatenate([q, extra], axis=1)
        q_out[here, :] = wide
        own_scores = jnp.where(causal, nt(q, own_keys), outside)
        scores = nt(wide, keys_ref[...])
        top = jnp.maximum(jnp.max(own_scores, axis=1, keepdims=True), jnp.max(scores, axis=1, keepdims=True))
        acc = nn(jnp.exp2((own_scores - top) * scale).astype(jnp.bfloat16), own_values)
        acc = acc + nn(jnp.exp2((scores - top) * scale).astype(jnp.bfloat16), values_ref[...])
        top_out[here, :] = jnp.broadcast_to(top, (rows, width))
        acc_out[here, :] = acc


def next_kernel(scale, heads, end, sizes, q_ref, own_ref, *refs):
    n_pieces = sum(sizes)
    piece_refs, refs = refs[:n_pieces], refs[n_pieces:]
    if end:
        top_in, acc_in, out_ref, keys_ref, values_ref, done_ref, sems = refs
    else:
        top_in, acc_in, top_out, acc_out, keys_ref, values_ref = refs
    rows, width = own_ref.shape[1], own_ref.shape[1] // 2
    first = ids_of(own_ref)[:, 0:1]
    level, at = jnp.zeros((1, 1), jnp.int32), 0
    for step, size in enumerate(sizes):
        matches = sum(count(ids_of(ref), first) for ref in piece_refs[at : at + size])
        level = jnp.where(matches > 0.0, step + 1, level)
        at += size
    level = level[0, 0]

    def go(n):
        for at, ref in enumerate(piece_refs[:n]):
            here = slice(at * rows, (at + 1) * rows)
            keys_ref[here, :] = wide_keys(ref, first, 1.0)
            values_ref[here, :] = wide_values(ref)
        copies = []

        def scores_of(head):
            return nt(q_ref[head * rows : (head + 1) * rows, :], keys_ref[0 : n * rows, :])

        ahead = scores_of(0) if n else None
        for head in range(heads):
            here = slice(head * rows, (head + 1) * rows)
            place = slice(head * width, (head + 1) * width)
            acc = acc_in[here, :]
            if n:
                scores = ahead
                before = top_in[here, 0:1]
                if head + 1 < heads:
                    ahead = scores_of(head + 1)
                top = jnp.maximum(before, jnp.max(scores, axis=1, keepdims=True))
                acc = acc * jnp.exp2((before - top) * scale)
                acc = acc + nn(jnp.exp2((scores - top) * scale).astype(jnp.bfloat16), values_ref[0 : n * rows, :])
            if end:
                done_ref[:, place] = (acc[:, 0:width] / acc[:, width:]).astype(jnp.bfloat16)
                copy = pltpu.make_async_copy(done_ref.at[:, place], out_ref.at[:, place], sems.at[head])
                copy.start()
                copies.append(copy)
            elif n:
                top_out[here, :] = jnp.broadcast_to(top, (rows, width))
                acc_out[here, :] = acc
        for copy in copies:
            copy.wait()

    if not end:
        return go(n_pieces)
    for step in range(len(sizes) + 1):
        pl.when(level == step)(functools.partial(go, sum(sizes[:step])))


def call(scale, heads, begin, end, q, own, sizes, pieces, state):
    vmem = pl.BlockSpec(memory_space=pltpu.VMEM)
    rows, width = own.shape[1], own.shape[1] // 2
    shape, f32, bf16 = jax.ShapeDtypeStruct, jnp.float32, jnp.bfloat16
    outs = [shape((heads * rows, width), f32), shape((heads * rows, 2 * width), f32)]
    kernel = functools.partial(next_kernel, scale, heads, end, sizes)
    if begin:
        outs.insert(0, shape((heads * rows, 2 * width), bf16))
        kernel = functools.partial(first_kernel, scale, heads)
    scratch = [pltpu.VMEM((len(pieces) * rows, 2 * width), bf16)] * 2
    out_specs = [vmem] * len(outs)
    if end:
        outs, out_specs = [shape((rows, heads * width), bf16)], [pl.BlockSpec(memory_space=pl.ANY)]
        scratch += [pltpu.VMEM((rows, heads * width), bf16), pltpu.SemaphoreType.DMA((heads,))]
    args = (q, own, *pieces, *state)
    moved = sum(math.prod(a.shape) * a.dtype.itemsize for a in (*args, *outs))
    flops = 8 * (len(pieces) + begin) * heads * rows * rows * width
    return pl.pallas_call(
        kernel,
        out_shape=outs,
        in_specs=[vmem] * len(args),
        out_specs=out_specs,
        scratch_shapes=scratch,
        cost_estimate=pl.CostEstimate(flops=flops, bytes_accessed=moved, transcendentals=flops // 512),
        compiler_params=pltpu.CompilerParams(vmem_limit_bytes=40 * 2**20),
    )(*args)


def body(queries, keys, values, doc_ids):
    heads = queries.shape[1] // keys.shape[1]
    scale = math.log2(math.e) / math.sqrt(keys.shape[1])
    kv0 = pack(keys, values, doc_ids)
    kv4 = chips_on(kv0, 4, True)
    kv2 = chips_on(kv0, 2, False)
    kv1 = chips_on(kv0, 1, True)
    kv3 = chips_on(kv4, -1, True)
    attend = functools.partial(call, scale, heads)

    def both(piece):
        return [piece, other_core(piece)]

    kv4t = other_core(kv4)
    q, *state = attend(True, False, queries, kv0, (2,), [other_core(kv0), kv4], [])
    q, state, kv1 = lax.optimization_barrier((q, state, kv1))
    state = attend(False, False, q, kv0, (2, 1), [*both(kv1), kv4t], state)
    (out,) = attend(False, True, q, kv0, (2, 2), [*both(kv2), *both(kv3)], state)
    return out


def solution(mesh):
    split_spec = P(axes, None)
    return jax.shard_map(
        body,
        mesh=mesh,
        in_specs=(split_spec, split_spec, split_spec, P(axes)),
        out_specs=split_spec,
        check_vma=False,
    )
```

```python
import functools
import math

import jax
import jax.numpy as jnp
from jax import lax
from jax.experimental import pallas as pl
from jax.experimental.pallas import tpu as pltpu
from jax.sharding import PartitionSpec as P

outside = -1e30
axes = ("dp", "context")
pad = 8


def chips_on(value, steps, wrap):
    count = lax.axis_size(axes[0]) * lax.axis_size(axes[1])
    shift = 2 * steps
    pairs = [(d, (d + shift) % count) for d in range(count)]
    return lax.ppermute(value, axes, [(a, b) for a, b in pairs if wrap or b == a + shift])


def other_core(value):
    count = lax.axis_size(axes[0]) * lax.axis_size(axes[1])
    return lax.ppermute(value, axes, [(d, d ^ 1) for d in range(count)])


def pack(keys, values, doc_ids):
    rows = keys.shape[0]
    packed = jnp.pad(jnp.concatenate([keys, values], axis=1), ((0, pad), (0, 0)))
    packed, doc_ids = lax.optimization_barrier((packed, doc_ids))
    ids = jnp.broadcast_to((doc_ids + 1).astype(jnp.bfloat16)[None, :], (pad, rows))
    return lax.dynamic_update_slice(packed, ids, (rows, 0))


def nt(a, b):
    return lax.dot_general(a, b, (((1,), (1,)), ((), ())), preferred_element_type=jnp.float32)


def nn(a, b):
    return lax.dot_general(a, b, (((1,), (0,)), ((), ())), preferred_element_type=jnp.float32)


def iotas(rows, columns):
    down = lax.broadcasted_iota(jnp.int32, (rows, columns), 0)
    across = lax.broadcasted_iota(jnp.int32, (rows, columns), 1)
    return down, across


def ids_of(ref):
    rows = ref.shape[1]
    return ref[rows : rows + 1, :].astype(jnp.float32)


def count(ids, wanted):
    return jnp.sum(jnp.where(ids == wanted, 1.0, 0.0), axis=1, keepdims=True)


def on_core_one():
    return jnp.where(lax.rem(lax.axis_index("context"), 2) == 1, 1.0, 0.0)


def causal_mask(own_ref):
    rows = own_ref.shape[1]
    ids = ids_of(own_ref)
    at_row, at_key = iotas(rows, rows)
    ids_col = jnp.sum(jnp.where(at_key == at_row, ids, 0.0), axis=1, keepdims=True)
    return (ids_col == ids) & (at_key <= at_row)


def wide_keys(ref, first, keep):
    rows, width = ref.shape[1], ref.shape[1] // 2
    matches = count(ids_of(ref), first) * keep
    down, across = iotas(rows, width)
    masked = jnp.where(down.astype(jnp.float32) >= rows - matches, 0.0, outside)
    extra = jnp.where(across == 0, masked, jnp.where(across == 1, 1.0, 0.0))
    return jnp.concatenate([ref[0:rows, 0:width], extra.astype(jnp.bfloat16)], axis=1)


def wide_values(ref):
    rows, width = ref.shape[1], ref.shape[1] // 2
    return jnp.concatenate([ref[0:rows, width : 2 * width], jnp.ones((rows, width), jnp.bfloat16)], axis=1)


def query_extra(ids, first, rows, width):
    down, across = iotas(rows, width)
    in_first = jnp.where(down.astype(jnp.float32) < count(ids, first), 0.0, outside)
    return jnp.where(across == 0, 1.0, jnp.where(across == 1, in_first, 0.0)).astype(jnp.bfloat16)


def raise_by(scores, top, scale):
    width = top.shape[1]
    parts = [scores[:, at : at + width] - top for at in range(0, scores.shape[1], width)]
    return jnp.concatenate([jnp.exp2(part * scale).astype(jnp.bfloat16) for part in parts], axis=1)


def first_kernel(scale, heads, q_ref, own_ref, *refs):
    *piece_refs, q_out, top_out, acc_out, keys_ref, values_ref = refs
    rows, width = own_ref.shape[1], own_ref.shape[1] // 2
    ids = ids_of(own_ref)
    first = ids[:, 0:1]
    causal = causal_mask(own_ref)
    own_keys, own_values = own_ref[0:rows, 0:width], wide_values(own_ref)
    extra = query_extra(ids, first, rows, width)
    for at, ref in enumerate(piece_refs):
        here = slice(at * rows, (at + 1) * rows)
        keys_ref[here, :] = wide_keys(ref, first, on_core_one() if at == 0 else 1.0)
        values_ref[here, :] = wide_values(ref)
    for head in range(heads):
        here = slice(head * rows, (head + 1) * rows)
        q = q_ref[:, head * width : (head + 1) * width]
        wide = jnp.concatenate([q, extra], axis=1)
        q_out[here, :] = wide
        own_scores = jnp.where(causal, nt(q, own_keys), outside)
        scores = nt(wide, keys_ref[...])
        top = jnp.maximum(jnp.max(own_scores, axis=1, keepdims=True), jnp.max(scores, axis=1, keepdims=True))
        acc = nn(jnp.exp2((own_scores - top) * scale).astype(jnp.bfloat16), own_values)
        acc = acc + nn(jnp.exp2((scores - top) * scale).astype(jnp.bfloat16), values_ref[...])
        top_out[here, :] = jnp.broadcast_to(top, (rows, width))
        acc_out[here, :] = acc


def next_kernel(scale, heads, end, sizes, q_ref, own_ref, *refs):
    n_pieces = sum(sizes)
    piece_refs, refs = refs[:n_pieces], refs[n_pieces:]
    if end:
        top_in, acc_in, out_ref, keys_ref, values_ref, done_ref, sems = refs
    else:
        top_in, acc_in, top_out, acc_out, keys_ref, values_ref = refs
    rows, width = own_ref.shape[1], own_ref.shape[1] // 2
    first = ids_of(own_ref)[:, 0:1]
    level, at = jnp.zeros((1, 1), jnp.int32), 0
    for step, size in enumerate(sizes):
        matches = sum(count(ids_of(ref), first) for ref in piece_refs[at : at + size])
        level = jnp.where(matches > 0.0, step + 1, level)
        at += size
    level = level[0, 0]

    def go(n):
        for at, ref in enumerate(piece_refs[:n]):
            here = slice(at * rows, (at + 1) * rows)
            keys_ref[here, :] = wide_keys(ref, first, 1.0)
            values_ref[here, :] = wide_values(ref)
        copies = []

        def scores_of(head):
            return nt(q_ref[head * rows : (head + 1) * rows, :], keys_ref[0 : n * rows, :])

        ahead = scores_of(0) if n else None
        for head in range(heads):
            here = slice(head * rows, (head + 1) * rows)
            place = slice(head * width, (head + 1) * width)
            acc = acc_in[here, :]
            if n:
                scores = ahead
                before = top_in[here, :]
                if head + 1 < heads:
                    ahead = scores_of(head + 1)
                top = jnp.maximum(before, jnp.max(scores, axis=1, keepdims=True))
                fade = jnp.exp2((before - top) * scale)
                acc = acc * jnp.concatenate([fade, fade], axis=1)
                acc = acc + nn(raise_by(scores, top, scale), values_ref[0 : n * rows, :])
            if end:
                done_ref[:, place] = (acc[:, 0:width] / acc[:, width:]).astype(jnp.bfloat16)
                copy = pltpu.make_async_copy(done_ref.at[:, place], out_ref.at[:, place], sems.at[head])
                copy.start()
                copies.append(copy)
            elif n:
                top_out[here, :] = top
                acc_out[here, :] = acc
        for copy in copies:
            copy.wait()

    if not end:
        return go(n_pieces)
    for step in range(len(sizes) + 1):
        pl.when(level == step)(functools.partial(go, sum(sizes[:step])))


def call(scale, heads, begin, end, q, own, sizes, pieces, state):
    vmem = pl.BlockSpec(memory_space=pltpu.VMEM)
    rows, width = own.shape[1], own.shape[1] // 2
    shape, f32, bf16 = jax.ShapeDtypeStruct, jnp.float32, jnp.bfloat16
    outs = [shape((heads * rows, width), f32), shape((heads * rows, 2 * width), f32)]
    kernel = functools.partial(next_kernel, scale, heads, end, sizes)
    if begin:
        outs.insert(0, shape((heads * rows, 2 * width), bf16))
        kernel = functools.partial(first_kernel, scale, heads)
    scratch = [pltpu.VMEM((len(pieces) * rows, 2 * width), bf16)] * 2
    out_specs = [vmem] * len(outs)
    if end:
        outs, out_specs = [shape((rows, heads * width), bf16)], [pl.BlockSpec(memory_space=pl.ANY)]
        scratch += [pltpu.VMEM((rows, heads * width), bf16), pltpu.SemaphoreType.DMA((heads,))]
    args = (q, own, *pieces, *state)
    moved = sum(math.prod(a.shape) * a.dtype.itemsize for a in (*args, *outs))
    flops = 8 * (len(pieces) + begin) * heads * rows * rows * width
    return pl.pallas_call(
        kernel,
        out_shape=outs,
        in_specs=[vmem] * len(args),
        out_specs=out_specs,
        scratch_shapes=scratch,
        cost_estimate=pl.CostEstimate(flops=flops, bytes_accessed=moved, transcendentals=flops // 512),
        compiler_params=pltpu.CompilerParams(vmem_limit_bytes=40 * 2**20),
    )(*args)


def body(queries, keys, values, doc_ids):
    heads = queries.shape[1] // keys.shape[1]
    scale = math.log2(math.e) / math.sqrt(keys.shape[1])
    kv0 = pack(keys, values, doc_ids)
    kv4 = chips_on(kv0, 4, True)
    kv2 = chips_on(kv0, 2, False)
    kv1 = chips_on(kv0, 1, True)
    kv3 = chips_on(kv4, -1, True)
    attend = functools.partial(call, scale, heads)

    def both(piece):
        return [piece, other_core(piece)]

    kv4t = other_core(kv4)
    q, *state = attend(True, False, queries, kv0, (2,), [other_core(kv0), kv4], [])
    q, state, kv1 = lax.optimization_barrier((q, state, kv1))
    state = attend(False, False, q, kv0, (2, 1), [*both(kv1), kv4t], state)
    (out,) = attend(False, True, q, kv0, (2, 2), [*both(kv2), *both(kv3)], state)
    return out


def solution(mesh):
    split_spec = P(axes, None)
    return jax.shard_map(
        body,
        mesh=mesh,
        in_specs=(split_spec, split_spec, split_spec, P(axes)),
        out_specs=split_spec,
        check_vma=False,
    )
```

```python
import functools
import math

import jax
import jax.numpy as jnp
from jax import lax
from jax.experimental import pallas as pl
from jax.experimental.pallas import tpu as pltpu
from jax.sharding import PartitionSpec as P

outside = -1e30
axes = ("dp", "context")
pad = 8


def chips_on(value, steps, wrap):
    count = lax.axis_size(axes[0]) * lax.axis_size(axes[1])
    shift = 2 * steps
    pairs = [(d, (d + shift) % count) for d in range(count)]
    return lax.ppermute(value, axes, [(a, b) for a, b in pairs if wrap or b == a + shift])


def other_core(value):
    count = lax.axis_size(axes[0]) * lax.axis_size(axes[1])
    return lax.ppermute(value, axes, [(d, d ^ 1) for d in range(count)])


def pack(keys, values, doc_ids):
    rows = keys.shape[0]
    packed = jnp.pad(jnp.concatenate([keys, values], axis=1), ((0, pad), (0, 0)))
    packed, doc_ids = lax.optimization_barrier((packed, doc_ids))
    ids = jnp.broadcast_to((doc_ids + 1).astype(jnp.bfloat16)[None, :], (pad, rows))
    return lax.dynamic_update_slice(packed, ids, (rows, 0))


def nt(a, b):
    return lax.dot_general(a, b, (((1,), (1,)), ((), ())), preferred_element_type=jnp.float32)


def nn(a, b):
    return lax.dot_general(a, b, (((1,), (0,)), ((), ())), preferred_element_type=jnp.float32)


def iotas(rows, columns):
    down = lax.broadcasted_iota(jnp.int32, (rows, columns), 0)
    across = lax.broadcasted_iota(jnp.int32, (rows, columns), 1)
    return down, across


def ids_of(ref):
    rows = ref.shape[1]
    return ref[rows : rows + 1, :].astype(jnp.float32)


def count(ids, wanted):
    return jnp.sum(jnp.where(ids == wanted, 1.0, 0.0), axis=1, keepdims=True)


def on_core_one():
    return jnp.where(lax.rem(lax.axis_index("context"), 2) == 1, 1.0, 0.0)


def causal_mask(own_ref):
    rows = own_ref.shape[1]
    ids = ids_of(own_ref)
    at_row, at_key = iotas(rows, rows)
    ids_col = jnp.sum(jnp.where(at_key == at_row, ids, 0.0), axis=1, keepdims=True)
    return (ids_col == ids) & (at_key <= at_row)


def wide_keys(ref, first, keep):
    rows, width = ref.shape[1], ref.shape[1] // 2
    matches = count(ids_of(ref), first) * keep
    down, across = iotas(rows, width)
    masked = jnp.where(down.astype(jnp.float32) >= rows - matches, 0.0, outside)
    extra = jnp.where(across == 0, masked, jnp.where(across == 1, 1.0, 0.0))
    return jnp.concatenate([ref[0:rows, 0:width], extra.astype(jnp.bfloat16)], axis=1)


def wide_values(ref):
    rows, width = ref.shape[1], ref.shape[1] // 2
    return jnp.concatenate([ref[0:rows, width : 2 * width], jnp.ones((rows, width), jnp.bfloat16)], axis=1)


def query_extra(ids, first, rows, width):
    down, across = iotas(rows, width)
    in_first = jnp.where(down.astype(jnp.float32) < count(ids, first), 0.0, outside)
    return jnp.where(across == 0, 1.0, jnp.where(across == 1, in_first, 0.0)).astype(jnp.bfloat16)


def raise_by(scores, top, scale):
    width = top.shape[1]
    parts = [scores[:, at : at + width] - top for at in range(0, scores.shape[1], width)]
    return jnp.concatenate([jnp.exp2(part * scale).astype(jnp.bfloat16) for part in parts], axis=1)


def first_kernel(scale, heads, q_ref, own_ref, *refs):
    *piece_refs, q_out, top_out, acc_out, keys_ref, values_ref = refs
    rows, width = own_ref.shape[1], own_ref.shape[1] // 2
    ids = ids_of(own_ref)
    first = ids[:, 0:1]
    causal = causal_mask(own_ref)
    own_keys, own_values = own_ref[0:rows, 0:width], wide_values(own_ref)
    extra = query_extra(ids, first, rows, width)
    for at, ref in enumerate(piece_refs):
        here = slice(at * rows, (at + 1) * rows)
        keys_ref[here, :] = wide_keys(ref, first, on_core_one() if at == 0 else 1.0)
        values_ref[here, :] = wide_values(ref)
    for head in range(heads):
        here = slice(head * rows, (head + 1) * rows)
        q = q_ref[:, head * width : (head + 1) * width]
        wide = jnp.concatenate([q, extra], axis=1)
        q_out[here, :] = wide
        own_scores = jnp.where(causal, nt(q, own_keys), outside)
        scores = nt(wide, keys_ref[...])
        top = jnp.maximum(jnp.max(own_scores, axis=1, keepdims=True), jnp.max(scores, axis=1, keepdims=True))
        acc = nn(jnp.exp2((own_scores - top) * scale).astype(jnp.bfloat16), own_values)
        acc = acc + nn(jnp.exp2((scores - top) * scale).astype(jnp.bfloat16), values_ref[...])
        top_out[here, :] = jnp.broadcast_to(top, (rows, width))
        acc_out[here, :] = acc


def next_kernel(scale, heads, end, sizes, q_ref, own_ref, *refs):
    n_pieces = sum(sizes)
    piece_refs, refs = refs[:n_pieces], refs[n_pieces:]
    if end:
        top_in, acc_in, out_ref, keys_ref, values_ref, done_ref, sems = refs
    else:
        top_in, acc_in, top_out, acc_out, keys_ref, values_ref = refs
    rows, width = own_ref.shape[1], own_ref.shape[1] // 2
    first = ids_of(own_ref)[:, 0:1]
    level, at = jnp.zeros((1, 1), jnp.int32), 0
    for step, size in enumerate(sizes):
        matches = sum(count(ids_of(ref), first) for ref in piece_refs[at : at + size])
        level = jnp.where(matches > 0.0, step + 1, level)
        at += size
    level = level[0, 0]

    def go(n):
        for at, ref in enumerate(piece_refs[:n]):
            here = slice(at * rows, (at + 1) * rows)
            keys_ref[here, :] = wide_keys(ref, first, 1.0)
            values_ref[here, :] = wide_values(ref)
        copies = []

        def scores_of(head):
            return nt(q_ref[head * rows : (head + 1) * rows, :], keys_ref[0 : n * rows, :])

        ahead = scores_of(0) if n else None
        for head in range(heads):
            here = slice(head * rows, (head + 1) * rows)
            place = slice(head * width, (head + 1) * width)
            acc = acc_in[here, :]
            if n:
                scores = ahead
                before = top_in[here, :]
                if head + 1 < heads:
                    ahead = scores_of(head + 1)
                top = jnp.maximum(before, jnp.max(scores, axis=1, keepdims=True))
                fade = jnp.exp2((before - top) * scale)
                acc = acc * jnp.concatenate([fade, fade], axis=1)
                acc = acc + nn(raise_by(scores, top, scale), values_ref[0 : n * rows, :])
            if end:
                done_ref[:, place] = (acc[:, 0:width] / acc[:, width:]).astype(jnp.bfloat16)
                copy = pltpu.make_async_copy(done_ref.at[:, place], out_ref.at[:, place], sems.at[head])
                copy.start()
                copies.append(copy)
            elif n:
                top_out[here, :] = top
                acc_out[here, :] = acc
        for copy in copies:
            copy.wait()

    if not end:
        return go(n_pieces)
    for step in range(len(sizes) + 1):
        pl.when(level == step)(functools.partial(go, sum(sizes[:step])))


def call(scale, heads, begin, end, q, own, sizes, pieces, state):
    vmem = pl.BlockSpec(memory_space=pltpu.VMEM)
    rows, width = own.shape[1], own.shape[1] // 2
    shape, f32, bf16 = jax.ShapeDtypeStruct, jnp.float32, jnp.bfloat16
    outs = [shape((heads * rows, width), f32), shape((heads * rows, 2 * width), f32)]
    kernel = functools.partial(next_kernel, scale, heads, end, sizes)
    if begin:
        outs.insert(0, shape((heads * rows, 2 * width), bf16))
        kernel = functools.partial(first_kernel, scale, heads)
    scratch = [pltpu.VMEM((len(pieces) * rows, 2 * width), bf16)] * 2
    out_specs = [vmem] * len(outs)
    if end:
        outs, out_specs = [shape((rows, heads * width), bf16)], [pl.BlockSpec(memory_space=pl.ANY)]
        scratch += [pltpu.VMEM((rows, heads * width), bf16), pltpu.SemaphoreType.DMA((heads,))]
    args = (q, own, *pieces, *state)
    moved = sum(math.prod(a.shape) * a.dtype.itemsize for a in (*args, *outs))
    flops = 8 * (len(pieces) + begin) * heads * rows * rows * width
    return pl.pallas_call(
        kernel,
        out_shape=outs,
        in_specs=[vmem] * len(args),
        out_specs=out_specs,
        scratch_shapes=scratch,
        cost_estimate=pl.CostEstimate(flops=flops, bytes_accessed=moved, transcendentals=flops // 512),
        compiler_params=pltpu.CompilerParams(vmem_limit_bytes=40 * 2**20),
    )(*args)


def body(queries, keys, values, doc_ids):
    heads = queries.shape[1] // keys.shape[1]
    scale = math.log2(math.e) / math.sqrt(keys.shape[1])
    kv0 = pack(keys, values, doc_ids)
    kv4 = chips_on(kv0, 4, True)
    kv2 = chips_on(kv0, 2, False)
    kv1 = chips_on(kv0, 1, True)
    kv3 = chips_on(kv4, -1, True)
    attend = functools.partial(call, scale, heads)

    def both(piece):
        return [piece, other_core(piece)]

    kv4t = other_core(kv4)
    q, *state = attend(True, False, queries, kv0, (2,), [other_core(kv0), kv4], [])
    q, state, kv1 = lax.optimization_barrier((q, state, kv1))
    state = attend(False, False, q, kv0, (2,), both(kv1), state)
    (out,) = attend(False, True, q, kv0, (2, 2, 1), [*both(kv2), *both(kv3), kv4t], state)
    return out


def solution(mesh):
    split_spec = P(axes, None)
    return jax.shard_map(
        body,
        mesh=mesh,
        in_specs=(split_spec, split_spec, split_spec, P(axes)),
        out_specs=split_spec,
        check_vma=False,
    )
```

```python
import functools
import math

import jax
import jax.numpy as jnp
from jax import lax
from jax.experimental import pallas as pl
from jax.experimental.pallas import tpu as pltpu
from jax.sharding import PartitionSpec as P

outside = -1e30
axes = ("dp", "context")
pad = 8


def chips_on(value, steps, wrap):
    count = lax.axis_size(axes[0]) * lax.axis_size(axes[1])
    shift = 2 * steps
    pairs = [(d, (d + shift) % count) for d in range(count)]
    return lax.ppermute(value, axes, [(a, b) for a, b in pairs if wrap or b == a + shift])


def other_core(value):
    count = lax.axis_size(axes[0]) * lax.axis_size(axes[1])
    return lax.ppermute(value, axes, [(d, d ^ 1) for d in range(count)])


def pack(keys, values, doc_ids):
    rows = keys.shape[0]
    packed = jnp.pad(jnp.concatenate([keys, values], axis=1), ((0, pad), (0, 0)))
    packed, doc_ids = lax.optimization_barrier((packed, doc_ids))
    ids = jnp.broadcast_to((doc_ids + 1).astype(jnp.bfloat16)[None, :], (pad, rows))
    return lax.dynamic_update_slice(packed, ids, (rows, 0))


def nt(a, b):
    return lax.dot_general(a, b, (((1,), (1,)), ((), ())), preferred_element_type=jnp.float32)


def nn(a, b):
    return lax.dot_general(a, b, (((1,), (0,)), ((), ())), preferred_element_type=jnp.float32)


def iotas(rows, columns):
    down = lax.broadcasted_iota(jnp.int32, (rows, columns), 0)
    across = lax.broadcasted_iota(jnp.int32, (rows, columns), 1)
    return down, across


def ids_of(ref):
    rows = ref.shape[1]
    return ref[rows : rows + 1, :].astype(jnp.float32)


def count(ids, wanted):
    return jnp.sum(jnp.where(ids == wanted, 1.0, 0.0), axis=1, keepdims=True)


def on_core_one():
    return jnp.where(lax.rem(lax.axis_index("context"), 2) == 1, 1.0, 0.0)


def causal_mask(own_ref):
    rows = own_ref.shape[1]
    ids = ids_of(own_ref)
    at_row, at_key = iotas(rows, rows)
    ids_col = jnp.sum(jnp.where(at_key == at_row, ids, 0.0), axis=1, keepdims=True)
    return (ids_col == ids) & (at_key <= at_row)


def wide_keys(ref, first, keep):
    rows, width = ref.shape[1], ref.shape[1] // 2
    matches = count(ids_of(ref), first) * keep
    down, across = iotas(rows, width)
    masked = jnp.where(down.astype(jnp.float32) >= rows - matches, 0.0, outside)
    extra = jnp.where(across == 0, masked, jnp.where(across == 1, 1.0, 0.0))
    return jnp.concatenate([ref[0:rows, 0:width], extra.astype(jnp.bfloat16)], axis=1)


def wide_values(ref):
    rows, width = ref.shape[1], ref.shape[1] // 2
    return jnp.concatenate([ref[0:rows, width : 2 * width], jnp.ones((rows, width), jnp.bfloat16)], axis=1)


def query_extra(ids, first, rows, width):
    down, across = iotas(rows, width)
    in_first = jnp.where(down.astype(jnp.float32) < count(ids, first), 0.0, outside)
    return jnp.where(across == 0, 1.0, jnp.where(across == 1, in_first, 0.0)).astype(jnp.bfloat16)


def raise_by(scores, top, scale):
    width = top.shape[1]
    parts = [scores[:, at : at + width] - top for at in range(0, scores.shape[1], width)]
    return jnp.concatenate([jnp.exp2(part * scale).astype(jnp.bfloat16) for part in parts], axis=1)


def first_kernel(scale, heads, q_ref, own_ref, *refs):
    *piece_refs, q_out, top_out, acc_out, keys_ref, values_ref = refs
    rows, width = own_ref.shape[1], own_ref.shape[1] // 2
    ids = ids_of(own_ref)
    first = ids[:, 0:1]
    causal = causal_mask(own_ref)
    own_keys, own_values = own_ref[0:rows, 0:width], wide_values(own_ref)
    extra = query_extra(ids, first, rows, width)
    for at, ref in enumerate(piece_refs):
        here = slice(at * rows, (at + 1) * rows)
        keys_ref[here, :] = wide_keys(ref, first, on_core_one() if at == 0 else 1.0)
        values_ref[here, :] = wide_values(ref)

    def scores_of(head):
        q = q_ref[:, head * width : (head + 1) * width]
        wide = jnp.concatenate([q, extra], axis=1)
        q_out[head * rows : (head + 1) * rows, :] = wide
        return nt(q, own_keys), nt(wide, keys_ref[...])

    ahead = scores_of(0)
    for head in range(heads):
        here = slice(head * rows, (head + 1) * rows)
        own_scores, scores = ahead
        if head + 1 < heads:
            ahead = scores_of(head + 1)
        own_scores = jnp.where(causal, own_scores, outside)
        top = jnp.maximum(jnp.max(own_scores, axis=1, keepdims=True), jnp.max(scores, axis=1, keepdims=True))
        acc = nn(jnp.exp2((own_scores - top) * scale).astype(jnp.bfloat16), own_values)
        acc = acc + nn(jnp.exp2((scores - top) * scale).astype(jnp.bfloat16), values_ref[...])
        top_out[here, :] = jnp.broadcast_to(top, (rows, width))
        acc_out[here, :] = acc


def next_kernel(scale, heads, end, sizes, q_ref, own_ref, *refs):
    n_pieces = sum(sizes)
    piece_refs, refs = refs[:n_pieces], refs[n_pieces:]
    if end:
        top_in, acc_in, out_ref, keys_ref, values_ref, done_ref, sems = refs
    else:
        top_in, acc_in, top_out, acc_out, keys_ref, values_ref = refs
    rows, width = own_ref.shape[1], own_ref.shape[1] // 2
    first = ids_of(own_ref)[:, 0:1]
    level, at = jnp.zeros((1, 1), jnp.int32), 0
    for step, size in enumerate(sizes):
        matches = sum(count(ids_of(ref), first) for ref in piece_refs[at : at + size])
        level = jnp.where(matches > 0.0, step + 1, level)
        at += size
    level = level[0, 0]

    def go(n):
        for at, ref in enumerate(piece_refs[:n]):
            here = slice(at * rows, (at + 1) * rows)
            keys_ref[here, :] = wide_keys(ref, first, 1.0)
            values_ref[here, :] = wide_values(ref)
        copies = []

        def scores_of(head):
            return nt(q_ref[head * rows : (head + 1) * rows, :], keys_ref[0 : n * rows, :])

        ahead = scores_of(0) if n else None
        for head in range(heads):
            here = slice(head * rows, (head + 1) * rows)
            place = slice(head * width, (head + 1) * width)
            acc = acc_in[here, :]
            if n:
                scores = ahead
                before = top_in[here, :]
                if head + 1 < heads:
                    ahead = scores_of(head + 1)
                top = jnp.maximum(before, jnp.max(scores, axis=1, keepdims=True))
                fade = jnp.exp2((before - top) * scale)
                acc = acc * jnp.concatenate([fade, fade], axis=1)
                acc = acc + nn(raise_by(scores, top, scale), values_ref[0 : n * rows, :])
            if end:
                done_ref[:, place] = (acc[:, 0:width] / acc[:, width:]).astype(jnp.bfloat16)
                copy = pltpu.make_async_copy(done_ref.at[:, place], out_ref.at[:, place], sems.at[head])
                copy.start()
                copies.append(copy)
            elif n:
                top_out[here, :] = top
                acc_out[here, :] = acc
        for copy in copies:
            copy.wait()

    if not end:
        return go(n_pieces)
    for step in range(len(sizes) + 1):
        pl.when(level == step)(functools.partial(go, sum(sizes[:step])))


def call(scale, heads, begin, end, q, own, sizes, pieces, state):
    vmem = pl.BlockSpec(memory_space=pltpu.VMEM)
    rows, width = own.shape[1], own.shape[1] // 2
    shape, f32, bf16 = jax.ShapeDtypeStruct, jnp.float32, jnp.bfloat16
    outs = [shape((heads * rows, width), f32), shape((heads * rows, 2 * width), f32)]
    kernel = functools.partial(next_kernel, scale, heads, end, sizes)
    if begin:
        outs.insert(0, shape((heads * rows, 2 * width), bf16))
        kernel = functools.partial(first_kernel, scale, heads)
    scratch = [pltpu.VMEM((len(pieces) * rows, 2 * width), bf16)] * 2
    out_specs = [vmem] * len(outs)
    if end:
        outs, out_specs = [shape((rows, heads * width), bf16)], [pl.BlockSpec(memory_space=pl.ANY)]
        scratch += [pltpu.VMEM((rows, heads * width), bf16), pltpu.SemaphoreType.DMA((heads,))]
    args = (q, own, *pieces, *state)
    moved = sum(math.prod(a.shape) * a.dtype.itemsize for a in (*args, *outs))
    flops = 8 * (len(pieces) + begin) * heads * rows * rows * width
    return pl.pallas_call(
        kernel,
        out_shape=outs,
        in_specs=[vmem] * len(args),
        out_specs=out_specs,
        scratch_shapes=scratch,
        cost_estimate=pl.CostEstimate(flops=flops, bytes_accessed=moved, transcendentals=flops // 512),
        compiler_params=pltpu.CompilerParams(vmem_limit_bytes=40 * 2**20),
    )(*args)


def body(queries, keys, values, doc_ids):
    heads = queries.shape[1] // keys.shape[1]
    scale = math.log2(math.e) / math.sqrt(keys.shape[1])
    kv0 = pack(keys, values, doc_ids)
    kv4 = chips_on(kv0, 4, True)
    kv2 = chips_on(kv0, 2, False)
    kv1 = chips_on(kv0, 1, True)
    kv3 = chips_on(kv4, -1, True)
    attend = functools.partial(call, scale, heads)

    def both(piece):
        return [piece, other_core(piece)]

    kv4t = other_core(kv4)
    q, *state = attend(True, False, queries, kv0, (2,), [other_core(kv0), kv4], [])
    q, state, kv1 = lax.optimization_barrier((q, state, kv1))
    state = attend(False, False, q, kv0, (2,), both(kv1), state)
    (out,) = attend(False, True, q, kv0, (2, 2, 1), [*both(kv2), *both(kv3), kv4t], state)
    return out


def solution(mesh):
    split_spec = P(axes, None)
    return jax.shard_map(
        body,
        mesh=mesh,
        in_specs=(split_spec, split_spec, split_spec, P(axes)),
        out_specs=split_spec,
        check_vma=False,
    )
```
